256 devices in a mesh: section: 16 (over z_lo, y), dp: 16 (over z_hi, x, core).
Axes of the slice: x: 4, y: 4, z: 8 (z_hi: 2, z_lo: 4; z = z_hi * 4 + z_lo), core: 2. Of those that a mesh axis runs over, the one named last changes fastest.
Arguments:
- inputs: bfloat16 [2048, 4096], P('dp', 'section'), may hold values from -0.3125 to 0.3125
- norm_gain: float32 [4096], P('section'), may hold values from 0.25 to 1.75
- router: bfloat16 [4096, 8], P('section'), may hold values from -0.09375 to 0.09375
- w_in: bfloat16 [16, 4096, 2, 6144], P('dp', None, None, 'section'), may hold values from -0.09375 to 0.09375
- w_out: bfloat16 [16, 6144, 4096], P('dp', 'section'), may hold values from -0.0546875 to 0.0546875
- routes: int32 [2048, 2], P('dp'), may hold values from 0 to 7, all different within a row; in each aligned block of 128 rows (0 to 127, 128 to 255, ...) at most 40 rows name the same one
Outputs:
- hiddens: bfloat16 [2048, 4096], P('dp', 'section')
The draws below stay inside these ranges and needn't reach their ends.
Inputs may be any that keep to these rules, and one draw needn't show every extreme that they name: `routes`: among the tokens of one index of dp (aligned blocks of 128 rows), no expert is named more than 40 times, a bound that some block reaches; a token's two experts differ.
All inputs are finite; a program needn't handle non-finite values.
Results may differ from the reference program's by a relative error of at most 0.0067.
Values may be sent and summed in bfloat16 or wider, within the bound.
No kernel may reach another device: no remote copies, remote signals or barrier semaphores. Data moves between devices by JAX's collectives and lax.ppermute only.
A program may use at most 128 MiB of HBM per device.

```python
import math
import jax
import jax.numpy as jnp
import numpy as np
from jax import lax

D = 4096
H = 12288
TOK_DEV = 128
EXPERTS = 8
TOKENS = 2048
CAP = 40
N_DP = 16


def shard_levels(key, dims, split, low, largest):
    def one(position, parts):
        draws = jax.random.uniform(jax.random.fold_in(jax.random.fold_in(key, 6), position), (parts,), jnp.float32, low / len(split), largest / len(split))
        return jnp.repeat(jnp.exp(draws), dims[position] // parts).reshape((-1,) + (1,) * (len(dims) - position - 1))

    gain = one(*split[0])
    for cut in split[1:]:
        gain = gain * one(*cut)
    return gain


def deal_out(key, own, number, rows, count, top, bound, skew):
    order = jax.random.permutation(key, count)
    crowded, usual = load_shares(count, rows * top, bound, skew, True), load_shares(count, rows * top, bound, skew, False)
    places = jnp.arange(count)

    def named(sizes, turn):
        used = int((sizes > 0).sum())
        fixed = max(1, used // 4)
        shifted = fixed + (places - fixed + turn * (used - fixed)) % max(1, count - fixed)
        return jnp.zeros((count,), jnp.int32).at[order[jnp.where(places < fixed, places, shifted)]].set(jnp.asarray(sizes, jnp.int32))

    sizes = jnp.where(number % 4 == 0, named(crowded, number // 4), named(usual, number - number // 4 - 1))
    mixed = jax.random.permutation(jax.random.fold_in(own, 3), count)
    donor, sink = mixed[0:count // 2 * 2:2], mixed[1:count // 2 * 2:2]
    margin = jnp.minimum(sizes[donor] - 1, bound - sizes[sink]) // 2
    margin = jnp.where((donor == order[0]) | (sink == order[0]) | (sizes[sink] == 0), 0, jnp.maximum(margin, 0))
    shifted = jax.random.randint(jax.random.fold_in(own, 4), (count // 2,), 0, 1 << 20) % (margin + 1)
    sizes = sizes.at[donor].add(-shifted).at[sink].add(shifted)
    labels = jnp.searchsorted(jnp.cumsum(sizes), jnp.arange(rows * top), side="right").astype(jnp.int32)
    listing = labels.reshape(top, rows).T
    listing = listing[jax.random.permutation(jax.random.fold_in(own, 1), rows)]
    turn = jax.random.randint(jax.random.fold_in(own, 2), (rows, 1), 0, top)
    return jnp.take_along_axis(listing, (jnp.arange(top)[None, :] + turn) % top, axis=1)


def load_shares(amount, total, reach, lean, full):
    portions = [(1 << 20) // math.isqrt(standing ** lean) + 1 for standing in range(1, amount + 1)]
    largest = reach if full else min(reach, max(-(-total // amount), total * portions[0] // sum(portions)))
    least = 1 if total - largest >= amount - 1 else 0
    counts, spare = [largest] + [least] * (amount - 1), total - largest - least * (amount - 1)
    while spare > 0:
        movable = [i for i in range(1, amount) if counts[i] < largest] or [i for i in range(1, amount) if counts[i] < reach]
        mass, remaining = sum([portions[i] for i in movable]), spare
        for i in movable:
            addition = min(reach - counts[i], max(1, remaining * portions[i] // mass), spare)
            counts[i] = counts[i] + addition
            spare = spare - addition
    return np.array(counts)


def scatter_about(key, extent, spread, bound, shards=(), kind=jnp.bfloat16):
    values = jax.random.normal(key, extent, jnp.float32) * spread
    if len(shards) > 0:
        values = shard_levels(key, extent, shards, -0.22, 0.18) * values
    return jnp.clip(values, min=-bound, max=bound).astype(kind)


def setup_inputs(seed: int = 0) -> dict:
    arg_keys = jax.random.split(jax.random.key(seed), 7)
    inputs = scatter_about(arg_keys[0], (TOKENS, D), 0.05, 0.3125, ((0, 16), (1, 16)))
    norm_gain = jnp.clip(1.0 + 0.15 * jax.random.normal(arg_keys[1], (D,), jnp.float32), 0.25, 1.75)
    router = scatter_about(arg_keys[2], (D, EXPERTS), D ** -0.5, 0.09375, ((0, 16),))
    w_in = scatter_about(arg_keys[3], (N_DP, D, 2, H // 2), D ** -0.5, 0.09375, ((0, 16), (3, 16)))
    w_out = scatter_about(arg_keys[4], (N_DP, H // 2, D), H ** -0.5, 0.0546875, ((0, 16), (1, 16)))
    routes_keys = jax.random.split(jax.random.fold_in(arg_keys[5], 1), TOKENS // TOK_DEV)
    routes_turns = jax.random.permutation(jax.random.fold_in(arg_keys[5], 3), TOKENS // TOK_DEV)
    routes = jax.vmap(lambda own, number: deal_out(jax.random.fold_in(arg_keys[5], 2), own, number, TOK_DEV, EXPERTS, 2, CAP, 2))(routes_keys, routes_turns).reshape((TOKENS, 2))
    return dict(inputs=inputs, norm_gain=norm_gain, router=router, w_in=w_in, w_out=w_out, routes=routes)


def slots_of(id_table, experts):
    flat_ids = id_table.reshape(-1)
    onehot = (flat_ids[:, None] == jnp.arange(experts, dtype=jnp.int32)[None, :]).astype(jnp.int32)
    ranked = jnp.cumsum(onehot, axis=0) - onehot
    return (flat_ids, lax.optimization_barrier(jnp.sum(ranked * onehot, axis=1)).astype(jnp.int32))

def reference(inputs, norm_gain, router, w_in, w_out, routes):
    acts_f32 = inputs.astype(jnp.float32)
    mean_square = lax.optimization_barrier(jnp.mean(acts_f32 * acts_f32, axis=-1, keepdims=True))
    normed = (acts_f32 * lax.rsqrt(mean_square + 1e-05) * norm_gain).astype(jnp.bfloat16)
    logits = jnp.dot(normed, router, preferred_element_type=jnp.float32)
    gate_probs = jax.nn.softmax(jnp.take_along_axis(logits, routes, axis=1), axis=1)
    expert_ids, slot_ids = jax.vmap(lambda table: slots_of(table, EXPERTS))(routes.reshape(N_DP, TOK_DEV, 2))
    global_slots = (slot_ids + jnp.arange(N_DP, dtype=jnp.int32)[:, None] * CAP).reshape(-1)
    expert_ids = expert_ids.reshape(-1)
    dup_rows = jnp.repeat(normed, 2, axis=0)
    buffer = jnp.zeros((EXPERTS, N_DP * CAP, D), jnp.bfloat16).at[expert_ids, global_slots].set(dup_rows)
    half_units = H // 2

    def piece_out(index):
        rows_in = lax.dynamic_index_in_dim(buffer, index // 2, 0, keepdims=False)
        w_rows = lax.dynamic_index_in_dim(w_in, index, 0, keepdims=False).reshape(D, H)
        w_down = lax.dynamic_index_in_dim(w_out, index, 0, keepdims=False)
        projection = jnp.dot(rows_in, w_rows, preferred_element_type=jnp.float32)
        hidden_act = (jax.nn.silu(projection[:, :half_units]) * projection[:, half_units:]).astype(jnp.bfloat16)
        return jnp.dot(hidden_act, w_down, preferred_element_type=jnp.float32)
    outputs = lax.map(piece_out, jnp.arange(N_DP, dtype=jnp.int32))
    summed_pairs = outputs.reshape(EXPERTS, 2, N_DP * CAP, D).sum(axis=1)
    picked = summed_pairs[expert_ids, global_slots].reshape(TOKENS, 2, D)
    return (acts_f32 + lax.optimization_barrier(jnp.sum(gate_probs[..., None] * picked, axis=1))).astype(jnp.bfloat16)
```

```python
import functools

import jax
import jax.numpy as jnp
from jax import lax
from jax.experimental import pallas as pl
from jax.experimental.pallas import tpu as pltpu
from jax.sharding import PartitionSpec as P

BF16 = jnp.bfloat16
F32 = jnp.float32

NZ, NY, NH, NX = 4, 4, 2, 4


def shift_y(value, step):
    pairs = [(z * NY + y, z * NY + (y + step) % NY) for z in range(NZ) for y in range(NY)]
    return lax.ppermute(value, "section", pairs)


def shift_z(value, step):
    pairs = [(z * NY + y, (z + step) % NZ * NY + y) for z in range(NZ) for y in range(NY)]
    return lax.ppermute(value, "section", pairs)


def xor_section(value, mask):
    return lax.ppermute(value, "section", [(s, s ^ mask) for s in range(NZ * NY)])


def shift_x(value, step):
    pairs = [
        ((h * NX + x) * 2 + c, (h * NX + (x + step) % NX) * 2 + c)
        for h in range(NH)
        for x in range(NX)
        for c in range(2)
    ]
    return lax.ppermute(value, "dp", pairs)


def swap_h(value):
    return lax.ppermute(value, "dp", [(d, d ^ (2 * NX)) for d in range(2 * NX * NH)])


def swap_core(value):
    return lax.ppermute(value, "dp", [(d, d ^ 1) for d in range(2 * NX * NH)])


def expert_kernel(
    place, g0, g1, g2a, g2b, g3, h0, h1, h2a, h2b, h3, w_up, w_down, own, other, rows, total
):
    zl, y = place[0], place[1]
    count = g0.shape[1]
    half = count // 2
    units = w_down.shape[0]
    width = g0.shape[2]
    for base, (p0, p1, p2a, p2b, p3) in ((0, (g0, g1, g2a, g2b, g3)), (count, (h0, h1, h2a, h2b, h3))):
        for d in range(NZ):
            z = (zl + d) % NZ
            for j, piece in ((0, p0), (1, p1), (3, p3)):
                rows[z * NY + (y + j) % NY, base : base + count] = piece[d]
            far = z * NY + (y + 2) % NY
            rows[far, base : base + half] = p2a[d]
            rows[far, base + half : base + count] = p2b[d]
    span = NY * width
    total[...] = jnp.zeros_like(total)

    def project(z, carry):
        left = jnp.concatenate([rows[z * NY + k] for k in range(NY)], axis=1)
        total[...] += jnp.dot(left, w_up[pl.ds(z * span, span), :], preferred_element_type=F32)
        return carry

    lax.fori_loop(0, NZ, project, 0)
    act = (jax.nn.silu(total[:, :units]) * total[:, units:]).astype(BF16)

    def expand(d, carry):
        z = (zl + d) % NZ
        for k in range(NY):
            start = pl.multiple_of(z * span + k * width, width)
            result = jnp.dot(act, w_down[:, pl.ds(start, width)], preferred_element_type=F32)
            j = (k - y + NY) % NY
            own[d, j] = result[:count]
            other[d, j] = result[count:].astype(BF16)
        return carry

    lax.fori_loop(0, NZ, expand, 0)


def expert(place, own_rows, other_rows, w_up, w_down):
    count, width = own_rows[0].shape[1:]
    shape = (NZ, NY, count, width)
    vmem = pl.BlockSpec(memory_space=pltpu.VMEM)
    return pl.pallas_call(
        expert_kernel,
        out_shape=(jax.ShapeDtypeStruct(shape, F32), jax.ShapeDtypeStruct(shape, BF16)),
        in_specs=[pl.BlockSpec(memory_space=pltpu.SMEM)] + [vmem] * 12,
        out_specs=(vmem, vmem),
        scratch_shapes=[
            pltpu.VMEM((NZ * NY, 2 * count, width), BF16),
            pltpu.VMEM((2 * count, w_up.shape[1]), F32),
        ],
        compiler_params=pltpu.CompilerParams(vmem_limit_bytes=48 * 1024 * 1024),
        cost_estimate=pl.CostEstimate(
            flops=6 * 2 * count * w_down.shape[0] * w_down.shape[1],
            bytes_accessed=16 * 1024 * 1024,
            transcendentals=2 * count * w_down.shape[0],
        ),
    )(place, *own_rows, *other_rows, w_up, w_down)


def gather_y(block):
    up = shift_y(block, -1)
    down = shift_y(block, 1)
    half = block.shape[1] // 2
    far_a = shift_y(down[:, :half], 1)
    far_b = shift_y(up[:, half:], -1)
    return block, up, far_a, far_b, down


def scatter_y(parts):
    half = parts.shape[2] // 2
    far_a = shift_y(parts[:, 2, :half].astype(BF16), 1)
    far_b = shift_y(parts[:, 2, half:].astype(BF16), -1)
    to_up = jnp.concatenate([parts[:, 1, :half] + far_a, parts[:, 1, half:]], axis=1).astype(BF16)
    to_down = jnp.concatenate([parts[:, 3, :half], parts[:, 3, half:] + far_b], axis=1).astype(BF16)
    return parts[:, 0] + shift_y(to_up, 1).astype(F32) + shift_y(to_down, -1).astype(F32)


def local(inputs, norm_gain, router, w_in, w_out, routes):
    sections = lax.axis_size("section")
    tokens, width = inputs.shape
    experts = router.shape[1]
    capacity = min(tokens, 5 * tokens // (2 * experts))
    units = w_out.shape[1]
    model = w_in.shape[1]
    section = lax.axis_index("section")
    dp = lax.axis_index("dp")
    zl, y = section // NY, section % NY
    zh, x = dp // (2 * NX), dp // 2 % NX
    w_up = w_in[0].reshape(model, 2 * units)
    w_down = w_out[0]

    acts = inputs.astype(F32)
    scaled = (acts * norm_gain).astype(BF16)
    partial_logits = lax.dot_general(
        router, scaled, (((0,), (1,)), ((), ())), preferred_element_type=F32
    )
    square = jnp.sum(acts * acts, axis=1)[None, :]
    sums = jnp.concatenate([square, partial_logits, jnp.zeros((7, tokens), F32)], axis=0)
    for mask in (1, 2, NY, 2 * NY):
        sums = sums + xor_section(sums, mask)
    inv = lax.rsqrt(sums[0] / model + 1e-05)
    logits = (sums[1 : 1 + experts] * inv[None, :]).T
    normed = (acts * inv[:, None] * norm_gain).astype(BF16)

    near = jnp.arange(experts, dtype=jnp.int32)
    names = (zh ^ (near // NX)) * NX + (x + near % NX) % NX
    hits = (routes[:, :, None] == names[None, None, :]).astype(F32)
    chosen = jnp.sum(hits, axis=1)
    earlier = (jnp.arange(tokens)[:, None] > jnp.arange(tokens)[None, :]).astype(F32)
    rank = jnp.dot(earlier, chosen, preferred_element_type=F32)
    slots = jnp.arange(capacity, dtype=F32)
    picks = chosen.T[:, None, :] * (rank.T[:, None, :] == slots[None, :, None]).astype(F32)
    picks = picks.reshape(experts * capacity, tokens)
    sent = jnp.dot(picks.astype(BF16), normed, preferred_element_type=F32).astype(BF16)
    sent = sent.reshape(NH, NX, capacity, width)

    crossed = jnp.stack([sent[0], swap_h(sent[1])], axis=1)
    arrived = [crossed[0]] + [shift_x(crossed[k], k) for k in range(1, NX)]
    mine = jnp.stack(arrived).reshape(experts * capacity, width)
    blocks = jnp.stack([mine] + [shift_z(mine, -d) for d in range(1, NZ)])
    own_rows = gather_y(blocks)
    other_rows = [swap_core(piece) for piece in own_rows]
    own, other = expert(jnp.stack([zl, y]).astype(jnp.int32), own_rows, other_rows, w_up, w_down)

    parts = own + swap_core(other).astype(F32)
    column = scatter_y(parts)
    full = column[0]
    for d in range(1, NZ):
        full = full + shift_z(column[d].astype(BF16), d).astype(F32)
    full = full.astype(BF16).reshape(NX, NH, capacity, width)
    back = jnp.stack([full[0]] + [shift_x(full[k], -k) for k in range(1, NX)])
    back = jnp.stack([back[:, 0], swap_h(back[:, 1])]).reshape(experts * capacity, width)

    named = (routes[:, :, None] == near[None, None, :]).astype(F32)
    pair = jnp.sum(named * logits[:, None, :], axis=2)
    gates = jax.nn.softmax(pair, axis=1)
    gate_of = jnp.sum(hits * gates[:, :, None], axis=1)
    weight = jnp.repeat(gate_of.T, capacity, axis=0) * picks
    high = weight.astype(BF16)
    low = (weight - high.astype(F32)).astype(BF16)
    mix = lambda w: lax.dot_general(w, back, (((0,), (0,)), ((), ())), preferred_element_type=F32)
    return (acts + (mix(high) + mix(low))).astype(BF16)


def solution(mesh):
    return jax.shard_map(
        local,
        mesh=mesh,
        in_specs=(
            P("dp", "section"),
            P("section"),
            P("section", None),
            P("dp", None, None, "section"),
            P("dp", "section", None),
            P("dp", None),
        ),
        out_specs=P("dp", "section"),
        check_vma=False,
    )
```

```python
import jax
import jax.numpy as jnp
from jax import lax
from jax.experimental import pallas as pl
from jax.experimental.pallas import tpu as pltpu
from jax.sharding import PartitionSpec as P

BF16 = jnp.bfloat16
F32 = jnp.float32

NZ, NY, NH, NX = 4, 4, 2, 4
GROUPS = ((0, 1), (2, 3))


def move(value, target):
    pairs = []
    for zl in range(NZ):
        for y in range(NY):
            for zh in range(NH):
                for x in range(NX):
                    for c in range(2):
                        a = ((zl * NY + y) * NH + zh) * NX * 2 + x * 2 + c
                        tz, ty, th, tx, tc = target(zl, y, zh, x, c)
                        b = ((tz * NY + ty) * NH + th) * NX * 2 + tx % NX * 2 + tc
                        pairs.append((a, b))
    return lax.ppermute(value, ("section", "dp"), pairs)


def shift_x(value, step):
    return move(value, lambda zl, y, zh, x, c: (zl, y, zh, x + step, c))


def xor_z(value, mask):
    return move(value, lambda zl, y, zh, x, c: (zl ^ mask, y, zh, x, c))


def xor_y(value, mask):
    return move(value, lambda zl, y, zh, x, c: (zl, y ^ mask, zh, x, c))


def far_y(value):
    return move(value, lambda zl, y, zh, x, c: (zl, y ^ (3 - 2 * c), zh, x, c))


def swap_h(value):
    return move(value, lambda zl, y, zh, x, c: (zl, y, zh ^ 1, x, c))


def swap_core(value):
    return move(value, lambda zl, y, zh, x, c: (zl, y, zh, x, c ^ 1))


def after(value, *others):
    return lax.optimization_barrier((value,) + others)[0]


def load(place, group, w_up, slab, sems):
    zl, y = place[0], place[1]
    copies = []
    for n, d in enumerate(group):
        for j in range(NY):
            start = pl.multiple_of(((zl ^ d) * NY + (y ^ j)) * WIDTH, WIDTH)
            copies.append(
                pltpu.make_async_copy(
                    w_up.at[pl.ds(start, WIDTH)],
                    slab.at[n, pl.ds(j * WIDTH, WIDTH)],
                    sems.at[n * NY + j],
                )
            )
    for copy in copies:
        copy.start()
    return copies


def square(blocks, squares, extras):
    count = squares.shape[0] // 2
    inverse = []
    sums = extras[...]
    for n in range(len(GROUPS[0])):
        for j in range(NY):
            extra = blocks[2 * j][n, count:].astype(F32)
            sums += extra
            inverse.append(1.0 / (extra[9:10] + extra[10:11] + extra[11:12]))
    extras[...] = sums
    step = 32

    def body(r, carry):
        start = pl.multiple_of(r * step, step)
        for side in range(2):
            place_at = pl.ds(pl.multiple_of(side * count + start, step), step)
            sums = squares[place_at, :]
            for n in range(len(GROUPS[0])):
                for j in range(NY):
                    plain = blocks[2 * j + side][n, pl.ds(start, step)].astype(F32)
                    plain = plain * inverse[n * NY + j]
                    sums += plain * plain
            squares[place_at, :] = sums
        return carry

    lax.fori_loop(0, count // step, body, 0)


def project(blocks, total, slab, copies):
    count = total.shape[0] // 2
    for n in range(len(GROUPS[0])):
        for copy in copies[n * NY : n * NY + NY] if copies else ():
            copy.wait()
        left = jnp.concatenate(
            [
                jnp.concatenate([blocks[2 * j + side][n, :count] for j in range(NY)], axis=1)
                for side in range(2)
            ],
            axis=0,
        )
        total[...] += jnp.dot(left, slab[n], preferred_element_type=F32)


def expand(place, act, w_down, own, give, group):
    zl, y = place[0], place[1]
    count = act.shape[0] // 2
    for n, d in enumerate(group):
        for j in range(NY):
            start = pl.multiple_of(((zl ^ d) * NY + (y ^ j)) * WIDTH, WIDTH)
            result = jnp.dot(act[...], w_down[:, pl.ds(start, WIDTH)], preferred_element_type=F32)
            own[j][n] = result[:count]
            give[j, n] = result[count:].astype(BF16)


def first_kernel(place, *refs):
    blocks, refs = refs[:8], refs[8:]
    w_up, w_down, total, squares, extras, next_slab, down, slab, sems, next_sems, sem = refs
    copies = load(place, GROUPS[0], w_up, slab, sems)
    later = load(place, GROUPS[1], w_up, next_slab, next_sems)
    whole = pltpu.make_async_copy(w_down, down, sem)
    whole.start()
    squares[...] = jnp.zeros_like(squares)
    extras[...] = jnp.zeros_like(extras)
    square(blocks, squares, extras)
    total[...] = jnp.zeros_like(total)
    project(blocks, total, slab, copies)
    for copy in later:
        copy.wait()
    whole.wait()


def second_kernel(place, *refs):
    blocks, refs = refs[:8], refs[8:]
    (total_in, squares_in, extras_in, slab, w_down, act), refs = refs[:6], refs[6:]
    own, (give, extras, total, squares) = refs[:NY], refs[NY:]
    units, model = w_down.shape
    total[...] = total_in[...]
    squares[...] = squares_in[...]
    extras[...] = extras_in[...]
    square(blocks, squares, extras)
    project(blocks, total, slab, None)
    mean = jnp.sum(squares[...], axis=1, keepdims=True) / model
    scale = lax.rsqrt(mean + 1e-05)
    act[...] = (jax.nn.silu(total[:, :units] * scale) * (total[:, units:] * scale)).astype(BF16)
    expand(place, act, w_down, own, give, GROUPS[1])


def third_kernel(place, act, w_down, *refs):
    expand(place, act, w_down, refs[:NY], refs[NY], GROUPS[0])


def call(kernel, out_shape, scratch, flops, remote, *args):
    vmem = pl.BlockSpec(memory_space=pltpu.VMEM)
    specs = [pl.BlockSpec(memory_space=pltpu.SMEM)] + [vmem] * (len(args) - 1)
    for k in range(len(args) - remote, len(args)):
        specs[k] = pl.BlockSpec(memory_space=pl.ANY)
    return pl.pallas_call(
        kernel,
        out_shape=out_shape,
        in_specs=specs,
        out_specs=(vmem,) * len(out_shape),
        scratch_shapes=scratch,
        compiler_params=pltpu.CompilerParams(vmem_limit_bytes=VMEM * 1024 * 1024),
        cost_estimate=pl.CostEstimate(flops=flops, bytes_accessed=8 * 1024 * 1024, transcendentals=0),
    )(*args)


VMEM = 24
WIDTH = 256


def shapes(blocks, units):
    count = blocks[0].shape[1] - 16
    totals = ((2 * count, 2 * units), (2 * count, WIDTH))
    slab = (len(GROUPS[0]), NY * WIDTH, 2 * units)
    return count, totals, slab, 4 * count * units * NZ * NY * WIDTH


def expert_first(place, blocks, w_up, w_down):
    shape = jax.ShapeDtypeStruct
    count, totals, slab, flops = shapes(blocks, w_down.shape[0])
    out = (shape(totals[0], F32), shape(totals[1], F32), shape((16, WIDTH), F32))
    out += (shape(slab, BF16), shape(w_down.shape, BF16))
    sems = pltpu.SemaphoreType.DMA((len(GROUPS[0]) * NY,))
    scratch = [pltpu.VMEM(slab, BF16), sems, sems, pltpu.SemaphoreType.DMA]
    return call(first_kernel, out, scratch, flops, 2, place, *blocks, w_up, w_down)


def expert_rest(place, blocks, state):
    shape = jax.ShapeDtypeStruct
    units = state[-1].shape[0]
    count, totals, slab, flops = shapes(blocks, units)
    part = (len(GROUPS[0]), count, WIDTH)
    sums = (shape(part, F32),) * NY + (shape((NY,) + part, BF16),)
    act, *second, extras = call(
        second_kernel,
        (shape((2 * count, units), BF16),) + sums + (shape((16, WIDTH), F32),),
        [pltpu.VMEM(t, F32) for t in totals],
        2 * flops,
        0,
        place,
        *blocks,
        *state,
    )
    first = call(third_kernel, sums, [], flops // 2, 0, place, act, state[-1])
    return first, second, extras


def split(value):
    high = lax.reduce_precision(value, 8, 7)
    return high.astype(BF16), (value - high).astype(BF16)


def slots(routes, names, capacity):
    tokens = routes.shape[0]
    chosen = jnp.sum((routes[:, :, None] == names[None, None, :]).astype(F32), axis=1)
    earlier = (jnp.arange(tokens)[:, None] > jnp.arange(tokens)[None, :]).astype(F32)
    rank = jnp.dot(earlier, chosen, preferred_element_type=F32)
    order = jnp.arange(capacity, dtype=F32)
    picks = chosen.T[:, None, :] * (rank.T[:, None, :] == order[None, :, None]).astype(F32)
    return picks.reshape(names.shape[0] * capacity, tokens)


def local(inputs, norm_gain, router, w_in, w_out, routes):
    tokens, width = inputs.shape
    experts = router.shape[1]
    capacity = min(tokens, 5 * tokens // (2 * experts))
    units = w_out.shape[1]
    model = w_in.shape[1]
    section = lax.axis_index("section")
    dp = lax.axis_index("dp")
    zl, y = section // NY, section % NY
    zh, x, core = dp // (2 * NX), dp // 2 % NX, dp % 2
    place = jnp.stack([zl, y]).astype(jnp.int32)
    w_down = w_out[0]

    acts = inputs.astype(F32)
    scaled = (acts * norm_gain).astype(BF16)
    named = jnp.zeros((16, width), BF16).at[:2, :tokens].set(routes.T.astype(BF16))
    partial_logits = lax.dot_general(
        router, scaled, (((0,), (1,)), ((), ())), preferred_element_type=F32
    )
    logit_rows = jnp.concatenate(split(partial_logits)).reshape(experts, width)
    square_row = jnp.concatenate(split(jnp.sum(acts * acts, axis=1)))[None, :]
    gain_high, _ = split(norm_gain)
    rest = norm_gain - gain_high.astype(F32)
    gain_rows = jnp.stack([gain_high, *split(rest)])
    extra = jnp.concatenate([logit_rows, square_row, gain_rows, jnp.zeros((4, width), BF16)])
    crossed = swap_h(jnp.concatenate([scaled, named], axis=0))
    near = (x + jnp.arange(NX, dtype=jnp.int32)) % NX
    names = jnp.concatenate([zh * NX + near, (zh ^ 1) * NX + near])
    picks = slots(routes, names, capacity)
    other_routes = crossed[tokens : tokens + 2, :tokens].T.astype(jnp.int32)
    other_picks = slots(other_routes, names[:NX], capacity)
    select = lambda p, v: jnp.dot(p.astype(BF16), v, preferred_element_type=F32).astype(BF16)
    mine = select(picks[: NX * capacity], scaled).reshape(NX, capacity, width)
    others = select(other_picks, crossed[:tokens]).reshape(NX, capacity, width)
    sent = jnp.stack([mine, others], axis=1)

    arrived = jnp.stack([sent[0]] + [shift_x(sent[k], k) for k in range(1, NX)])
    arrived = jnp.concatenate([arrived.reshape(NX * NH * capacity, width), extra])
    spread = [arrived] + [xor_z(arrived, d) for d in range(1, NZ)]
    blocks = []
    for group in GROUPS:
        own = jnp.stack([spread[d] for d in group])
        one, three = xor_y(own, 1), xor_y(own, 3)
        turn = jnp.where(core == 0, one, three)
        if group is GROUPS[0]:
            w_up = after(w_in, arrived)[0].reshape(model, 2 * units)
        far = far_y(turn)
        for piece in (own, one, far, three):
            if group is not GROUPS[0]:
                piece = after(piece, state[0])
            blocks += [piece, swap_core(piece)]
        if group is GROUPS[0]:
            state = expert_first(place, blocks, w_up, w_down)

    first, second, extras = expert_rest(place, blocks[8:], state)
    results = (first, second)
    sums = (extras[:4] + extras[4:8]).reshape(experts, tokens)
    inverse = lax.rsqrt((extras[8, :tokens] + extras[8, tokens:]) / model + 1e-05)
    logits = (sums * inverse[None, :]).T

    terms = [None] * NZ
    for g in (1, 0):
        *own, give = results[g]
        given = swap_core(give)
        parts = [own[j] + given[j].astype(F32) for j in range(NY)]
        passed = far_y(parts[2].astype(BF16)).astype(F32)
        one = xor_y((parts[1] + jnp.where(core == 0, passed, 0.0)).astype(BF16), 1)
        three = xor_y((parts[3] + jnp.where(core == 0, 0.0, passed)).astype(BF16), 3)
        column = parts[0] + one.astype(F32) + three.astype(F32)
        for n, d in enumerate(GROUPS[g]):
            terms[d] = xor_z(column[n].astype(BF16), d).astype(F32) if d else column[n]
    full = sum(terms[1:], terms[0]).astype(BF16).reshape(NX, NH, capacity, width)
    back = jnp.stack([full[0]] + [shift_x(full[k], -k) for k in range(1, NX)], axis=1)
    back = jnp.concatenate([back[0], swap_h(back[1])]).reshape(experts * capacity, width)

    hits = (routes[:, :, None] == names[None, None, :]).astype(F32)
    table = (routes[:, :, None] == jnp.arange(experts)[None, None, :]).astype(F32)
    gates = jax.nn.softmax(jnp.sum(table * logits[:, None, :], axis=2), axis=1)
    gate_of = jnp.sum(hits * gates[:, :, None], axis=1)
    weight = jnp.repeat(gate_of.T, capacity, axis=0) * picks
    high, low = split(weight)
    mix = lambda w: lax.dot_general(w, back, (((0,), (0,)), ((), ())), preferred_element_type=F32)
    return (acts + (mix(high) + mix(low))).astype(BF16)


def solution(mesh):
    return jax.shard_map(
        local,
        mesh=mesh,
        in_specs=(
            P("dp", "section"),
            P("section"),
            P("section", None),
            P("dp", None, None, "section"),
            P("dp", "section", None),
            P("dp", None),
        ),
        out_specs=P("dp", "section"),
        check_vma=False,
    )
```

```python
import jax
import jax.numpy as jnp
from jax import lax
from jax.experimental import pallas as pl
from jax.experimental.pallas import tpu as pltpu
from jax.sharding import PartitionSpec as P

BF16 = jnp.bfloat16
F32 = jnp.float32

NZ, NY, NH, NX = 4, 4, 2, 4
GROUPS = ((0, 1), (2, 3))


def move(value, target):
    pairs = []
    for zl in range(NZ):
        for y in range(NY):
            for zh in range(NH):
                for x in range(NX):
                    for c in range(2):
                        a = ((zl * NY + y) * NH + zh) * NX * 2 + x * 2 + c
                        tz, ty, th, tx, tc = target(zl, y, zh, x, c)
                        b = ((tz * NY + ty) * NH + th) * NX * 2 + tx % NX * 2 + tc
                        pairs.append((a, b))
    return lax.ppermute(value, ("section", "dp"), pairs)


def shift_x(value, step):
    return move(value, lambda zl, y, zh, x, c: (zl, y, zh, x + step, c))


def xor_z(value, mask):
    return move(value, lambda zl, y, zh, x, c: (zl ^ mask, y, zh, x, c))


def xor_y(value, mask):
    return move(value, lambda zl, y, zh, x, c: (zl, y ^ mask, zh, x, c))


def far_y(value):
    return move(value, lambda zl, y, zh, x, c: (zl, y ^ (3 - 2 * c), zh, x, c))


def swap_h(value):
    return move(value, lambda zl, y, zh, x, c: (zl, y, zh ^ 1, x, c))


def swap_core(value):
    return move(value, lambda zl, y, zh, x, c: (zl, y, zh, x, c ^ 1))


def after(value, *others):
    return lax.optimization_barrier((value,) + others)[0]


def load(place, group, w_up, slab, sems):
    zl, y = place[0], place[1]
    copies = []
    for n, d in enumerate(group):
        for j in range(NY):
            start = pl.multiple_of(((zl ^ d) * NY + (y ^ j)) * WIDTH, WIDTH)
            copies.append(
                pltpu.make_async_copy(
                    w_up.at[pl.ds(start, WIDTH)],
                    slab.at[n, pl.ds(j * WIDTH, WIDTH)],
                    sems.at[n * NY + j],
                )
            )
    for copy in copies:
        copy.start()
    return copies


def square(blocks, squares, extras):
    count = squares.shape[0] // 2
    inverse = []
    sums = extras[...]
    for n in range(len(GROUPS[0])):
        for j in range(NY):
            extra = blocks[2 * j][n, count:].astype(F32)
            sums += extra
            inverse.append(1.0 / (extra[9:10] + extra[10:11] + extra[11:12]))
    extras[...] = sums
    step = 32

    def body(r, carry):
        start = pl.multiple_of(r * step, step)
        for side in range(2):
            place_at = pl.ds(pl.multiple_of(side * count + start, step), step)
            sums = squares[place_at, :]
            for n in range(len(GROUPS[0])):
                for j in range(NY):
                    plain = blocks[2 * j + side][n, pl.ds(start, step)].astype(F32)
                    plain = plain * inverse[n * NY + j]
                    sums += plain * plain
            squares[place_at, :] = sums
        return carry

    lax.fori_loop(0, count // step, body, 0)


def project(blocks, total, slab, copies):
    count = total.shape[0] // 2
    for n in range(len(GROUPS[0])):
        for copy in copies[n * NY : n * NY + NY] if copies else ():
            copy.wait()
        left = jnp.concatenate(
            [
                jnp.concatenate([blocks[2 * j + side][n, :count] for j in range(NY)], axis=1)
                for side in range(2)
            ],
            axis=0,
        )
        total[...] += jnp.dot(left, slab[n], preferred_element_type=F32)


def arrange(place, blocks, rows, inverse, extras):
    zl, y = place[0], place[1]
    count = blocks[0].shape[1] - 16
    sums = extras[...]
    for j in range(NY):
        for n in range(2):
            k = ((zl ^ n) % 2) * NY + (y ^ j)
            rows[k, :count] = blocks[2 * j][n, :count]
            rows[k, count:] = blocks[2 * j + 1][n, :count]
            extra = blocks[2 * j][n, count:].astype(F32)
            sums += extra
            inverse[pl.ds(k, 1), :] = 1.0 / (extra[9:10] + extra[10:11] + extra[11:12])
    extras[...] = sums


def near_square(rows, inverse, squares):
    step = 32

    def body(r, carry):
        at = pl.ds(pl.multiple_of(r * step, step), step)
        sums = squares[at, :]
        for k in range(2 * NY):
            plain = rows[k, at, :].astype(F32) * inverse[k : k + 1, :]
            sums += plain * plain
        squares[at, :] = sums
        return carry

    lax.fori_loop(0, rows.shape[1] // step, body, 0)


def near_project(rows, w_up, first):
    left = jnp.concatenate([rows[k] for k in range(2 * NY)], axis=1)
    start = pl.multiple_of(first * (2 * NY * WIDTH), 2 * NY * WIDTH)
    return jnp.dot(left, w_up[pl.ds(start, 2 * NY * WIDTH), :], preferred_element_type=F32)


def expand(place, act, w_down, own, give, group):
    zl, y = place[0], place[1]
    count = act.shape[0] // 2
    for n, d in enumerate(group):
        for j in range(NY):
            start = pl.multiple_of(((zl ^ d) * NY + (y ^ j)) * WIDTH, WIDTH)
            result = jnp.dot(act[...], w_down[:, pl.ds(start, WIDTH)], preferred_element_type=F32)
            own[j][n] = result[:count]
            give[j, n] = result[count:].astype(BF16)


def first_kernel(place, *refs):
    blocks, refs = refs[: 2 * NY], refs[2 * NY :]
    w_up, w_down, total, squares, extras, next_slab, down, rows, inverse, sems, sem = refs
    later = load(place, GROUPS[1], w_up, next_slab, sems)
    whole = pltpu.make_async_copy(w_down, down, sem)
    whole.start()
    squares[...] = jnp.zeros_like(squares)
    extras[...] = jnp.zeros_like(extras)
    arrange(place, blocks, rows, inverse, extras)
    total[...] = near_project(rows, w_up, place[0] // 2)
    near_square(rows, inverse, squares)
    for copy in later:
        copy.wait()
    whole.wait()


def second_kernel(place, *refs):
    blocks, refs = refs[:8], refs[8:]
    (total_in, squares_in, extras_in, slab, w_down, act), refs = refs[:6], refs[6:]
    own, (give, extras, total, squares) = refs[:NY], refs[NY:]
    units, model = w_down.shape
    total[...] = total_in[...]
    squares[...] = squares_in[...]
    extras[...] = extras_in[...]
    square(blocks, squares, extras)
    project(blocks, total, slab, None)
    mean = jnp.sum(squares[...], axis=1, keepdims=True) / model
    scale = lax.rsqrt(mean + 1e-05)
    act[...] = (jax.nn.silu(total[:, :units] * scale) * (total[:, units:] * scale)).astype(BF16)
    expand(place, act, w_down, own, give, GROUPS[1])


def third_kernel(place, act, w_down, *refs):
    expand(place, act, w_down, refs[:NY], refs[NY], GROUPS[0])


def call(kernel, out_shape, scratch, flops, remote, *args):
    vmem = pl.BlockSpec(memory_space=pltpu.VMEM)
    specs = [pl.BlockSpec(memory_space=pltpu.SMEM)] + [vmem] * (len(args) - 1)
    if remote:
        specs[-1] = pl.BlockSpec(memory_space=pl.ANY)
    return pl.pallas_call(
        kernel,
        out_shape=out_shape,
        in_specs=specs,
        out_specs=(vmem,) * len(out_shape),
        scratch_shapes=scratch,
        compiler_params=pltpu.CompilerParams(vmem_limit_bytes=VMEM * 1024 * 1024),
        cost_estimate=pl.CostEstimate(flops=flops, bytes_accessed=8 * 1024 * 1024, transcendentals=0),
    )(*args)


VMEM = 24
WIDTH = 256


def shapes(blocks, units):
    count = blocks[0].shape[1] - 16
    totals = ((2 * count, 2 * units), (2 * count, WIDTH))
    slab = (len(GROUPS[0]), NY * WIDTH, 2 * units)
    return count, totals, slab, 4 * count * units * NZ * NY * WIDTH


def expert_first(place, blocks, w_up, w_down):
    shape = jax.ShapeDtypeStruct
    count, totals, slab, flops = shapes(blocks, w_down.shape[0])
    out = (shape(totals[0], F32), shape(totals[1], F32), shape((16, WIDTH), F32))
    out += (shape(slab, BF16), shape(w_down.shape, BF16))
    sems = pltpu.SemaphoreType.DMA((len(GROUPS[0]) * NY,))
    scratch = [pltpu.VMEM((2 * NY, 2 * count, WIDTH), BF16), pltpu.VMEM((2 * NY, WIDTH), F32)]
    scratch += [sems, pltpu.SemaphoreType.DMA]
    return call(first_kernel, out, scratch, flops, True, place, *blocks, w_up, w_down)


def expert_rest(place, blocks, state):
    shape = jax.ShapeDtypeStruct
    units = state[-1].shape[0]
    count, totals, slab, flops = shapes(blocks, units)
    part = (len(GROUPS[0]), count, WIDTH)
    sums = (shape(part, F32),) * NY + (shape((NY,) + part, BF16),)
    act, *second, extras = call(
        second_kernel,
        (shape((2 * count, units), BF16),) + sums + (shape((16, WIDTH), F32),),
        [pltpu.VMEM(t, F32) for t in totals],
        2 * flops,
        False,
        place,
        *blocks,
        *state,
    )
    first = call(third_kernel, sums, [], flops // 2, False, place, act, state[-1])
    return first, second, extras


def split(value):
    high = lax.reduce_precision(value, 8, 7)
    return high.astype(BF16), (value - high).astype(BF16)


def slots(routes, names, capacity):
    tokens = routes.shape[0]
    chosen = jnp.sum((routes[:, :, None] == names[None, None, :]).astype(F32), axis=1)
    earlier = (jnp.arange(tokens)[:, None] > jnp.arange(tokens)[None, :]).astype(F32)
    rank = jnp.dot(earlier, chosen, preferred_element_type=F32)
    order = jnp.arange(capacity, dtype=F32)
    picks = chosen.T[:, None, :] * (rank.T[:, None, :] == order[None, :, None]).astype(F32)
    return picks.reshape(names.shape[0] * capacity, tokens)


def local(inputs, norm_gain, router, w_in, w_out, routes):
    tokens, width = inputs.shape
    experts = router.shape[1]
    capacity = min(tokens, 5 * tokens // (2 * experts))
    units = w_out.shape[1]
    model = w_in.shape[1]
    section = lax.axis_index("section")
    dp = lax.axis_index("dp")
    zl, y = section // NY, section % NY
    zh, x, core = dp // (2 * NX), dp // 2 % NX, dp % 2
    place = jnp.stack([zl, y]).astype(jnp.int32)
    w_down = w_out[0]

    acts = inputs.astype(F32)
    scaled = (acts * norm_gain).astype(BF16)
    named = jnp.zeros((16, width), BF16).at[:2, :tokens].set(routes.T.astype(BF16))
    partial_logits = lax.dot_general(
        router, scaled, (((0,), (1,)), ((), ())), preferred_element_type=F32
    )
    logit_rows = jnp.concatenate(split(partial_logits)).reshape(experts, width)
    square_row = jnp.concatenate(split(jnp.sum(acts * acts, axis=1)))[None, :]
    gain_high, _ = split(norm_gain)
    rest = norm_gain - gain_high.astype(F32)
    gain_rows = jnp.stack([gain_high, *split(rest)])
    extra = jnp.concatenate([logit_rows, square_row, gain_rows, jnp.zeros((4, width), BF16)])
    crossed = swap_h(jnp.concatenate([scaled, named], axis=0))
    near = (x + jnp.arange(NX, dtype=jnp.int32)) % NX
    names = jnp.concatenate([zh * NX + near, (zh ^ 1) * NX + near])
    picks = slots(routes, names, capacity)
    other_routes = crossed[tokens : tokens + 2, :tokens].T.astype(jnp.int32)
    other_picks = slots(other_routes, names[:NX], capacity)
    select = lambda p, v: jnp.dot(p.astype(BF16), v, preferred_element_type=F32).astype(BF16)
    mine = select(picks[: NX * capacity], scaled).reshape(NX, capacity, width)
    others = select(other_picks, crossed[:tokens]).reshape(NX, capacity, width)
    sent = jnp.stack([mine, others], axis=1)

    arrived = jnp.stack([sent[0]] + [shift_x(sent[k], k) for k in range(1, NX)])
    arrived = jnp.concatenate([arrived.reshape(NX * NH * capacity, width), extra])
    spread = [arrived] + [xor_z(arrived, d) for d in range(1, NZ)]
    blocks = []
    for group in GROUPS:
        own = jnp.stack([spread[d] for d in group])
        one, three = xor_y(own, 1), xor_y(own, 3)
        turn = jnp.where(core == 0, one, three)
        if group is GROUPS[0]:
            w_up = after(w_in, arrived)[0].reshape(model, 2 * units)
        far = far_y(turn)
        for piece in (own, one, far, three):
            if group is not GROUPS[0]:
                piece = after(piece, state[0])
            blocks += [piece, swap_core(piece)]
        if group is GROUPS[0]:
            state = expert_first(place, blocks, w_up, w_down)

    first, second, extras = expert_rest(place, blocks[8:], state)
    results = (first, second)
    sums = (extras[:4] + extras[4:8]).reshape(experts, tokens)
    inverse = lax.rsqrt((extras[8, :tokens] + extras[8, tokens:]) / model + 1e-05)
    logits = (sums * inverse[None, :]).T

    terms = [None] * NZ
    for g in (1, 0):
        *own, give = results[g]
        given = swap_core(give)
        parts = [own[j] + given[j].astype(F32) for j in range(NY)]
        passed = far_y(parts[2].astype(BF16)).astype(F32)
        one = xor_y((parts[1] + jnp.where(core == 0, passed, 0.0)).astype(BF16), 1)
        three = xor_y((parts[3] + jnp.where(core == 0, 0.0, passed)).astype(BF16), 3)
        column = parts[0] + one.astype(F32) + three.astype(F32)
        for n, d in enumerate(GROUPS[g]):
            terms[d] = xor_z(column[n].astype(BF16), d).astype(F32) if d else column[n]
    full = sum(terms[1:], terms[0]).astype(BF16).reshape(NX, NH, capacity, width)
    back = jnp.stack([full[0]] + [shift_x(full[k], -k) for k in range(1, NX)], axis=1)
    back = jnp.concatenate([back[0], swap_h(back[1])]).reshape(experts * capacity, width)

    hits = (routes[:, :, None] == names[None, None, :]).astype(F32)
    table = (routes[:, :, None] == jnp.arange(experts)[None, None, :]).astype(F32)
    gates = jax.nn.softmax(jnp.sum(table * logits[:, None, :], axis=2), axis=1)
    gate_of = jnp.sum(hits * gates[:, :, None], axis=1)
    weight = jnp.repeat(gate_of.T, capacity, axis=0) * picks
    high, low = split(weight)
    mix = lambda w: lax.dot_general(w, back, (((0,), (0,)), ((), ())), preferred_element_type=F32)
    return (acts + (mix(high) + mix(low))).astype(BF16)


def solution(mesh):
    return jax.shard_map(
        local,
        mesh=mesh,
        in_specs=(
            P("dp", "section"),
            P("section"),
            P("section", None),
            P("dp", None, None, "section"),
            P("dp", "section", None),
            P("dp", None),
        ),
        out_specs=P("dp", "section"),
        check_vma=False,
    )
```

```python
import jax
import jax.numpy as jnp
from jax import lax
from jax.experimental import pallas as pl
from jax.experimental.pallas import tpu as pltpu
from jax.sharding import PartitionSpec as P

BF16 = jnp.bfloat16
F32 = jnp.float32

NZ, NY, NH, NX = 4, 4, 2, 4
GROUPS = ((0, 1), (2, 3))


def move(value, target):
    pairs = []
    for zl in range(NZ):
        for y in range(NY):
            for zh in range(NH):
                for x in range(NX):
                    for c in range(2):
                        a = ((zl * NY + y) * NH + zh) * NX * 2 + x * 2 + c
                        tz, ty, th, tx, tc = target(zl, y, zh, x, c)
                        b = ((tz * NY + ty) * NH + th) * NX * 2 + tx % NX * 2 + tc
                        pairs.append((a, b))
    return lax.ppermute(value, ("section", "dp"), pairs)


def shift_x(value, step):
    return move(value, lambda zl, y, zh, x, c: (zl, y, zh, x + step, c))


def xor_z(value, mask):
    return move(value, lambda zl, y, zh, x, c: (zl ^ mask, y, zh, x, c))


def xor_y(value, mask):
    return move(value, lambda zl, y, zh, x, c: (zl, y ^ mask, zh, x, c))


def far_y(value):
    return move(value, lambda zl, y, zh, x, c: (zl, y ^ (3 - 2 * c), zh, x, c))


def swap_h(value):
    return move(value, lambda zl, y, zh, x, c: (zl, y, zh ^ 1, x, c))


def swap_core(value):
    return move(value, lambda zl, y, zh, x, c: (zl, y, zh, x, c ^ 1))


def after(value, *others):
    return lax.optimization_barrier((value,) + others)[0]


def load(place, group, w_up, slab, sems):
    zl, y = place[0], place[1]
    copies = []
    for n, d in enumerate(group):
        for j in range(NY):
            start = pl.multiple_of(((zl ^ d) * NY + (y ^ j)) * WIDTH, WIDTH)
            copies.append(
                pltpu.make_async_copy(
                    w_up.at[pl.ds(start, WIDTH)],
                    slab.at[n, pl.ds(j * WIDTH, WIDTH)],
                    sems.at[n * NY + j],
                )
            )
    for copy in copies:
        copy.start()
    return copies


def square(blocks, squares, extras):
    count = squares.shape[0] // 2
    inverse = []
    sums = extras[...]
    for n in range(len(GROUPS[0])):
        for j in range(NY):
            extra = blocks[2 * j][n, count:].astype(F32)
            sums += extra
            inverse.append(1.0 / (extra[9:10] + extra[10:11] + extra[11:12]))
    extras[...] = sums
    step = 32

    def body(r, carry):
        start = pl.multiple_of(r * step, step)
        for side in range(2):
            place_at = pl.ds(pl.multiple_of(side * count + start, step), step)
            sums = squares[place_at, :]
            for n in range(len(GROUPS[0])):
                for j in range(NY):
                    plain = blocks[2 * j + side][n, pl.ds(start, step)].astype(F32)
                    plain = plain * inverse[n * NY + j]
                    sums += plain * plain
            squares[place_at, :] = sums
        return carry

    lax.fori_loop(0, count // step, body, 0)


def part_of(blocks, n, slab):
    count = blocks[0].shape[1] - 16
    sides = [
        jnp.concatenate([blocks[2 * j + side][n, :count] for j in range(NY)], axis=1)
        for side in range(2)
    ]
    return jnp.dot(jnp.concatenate(sides, axis=0), slab[n], preferred_element_type=F32)


def arrange(place, blocks, rows, inverse, extras):
    zl, y = place[0], place[1]
    count = blocks[0].shape[1] - 16
    sums = extras[...]
    for j in range(NY):
        for n in range(2):
            k = ((zl ^ n) % 2) * NY + (y ^ j)
            rows[k, :count] = blocks[2 * j][n, :count]
            rows[k, count:] = blocks[2 * j + 1][n, :count]
            extra = blocks[2 * j][n, count:].astype(F32)
            sums += extra
            inverse[pl.ds(k, 1), :] = 1.0 / (extra[9:10] + extra[10:11] + extra[11:12])
    extras[...] = sums


def near_square(rows, inverse, squares):
    step = 32

    def body(r, carry):
        at = pl.ds(pl.multiple_of(r * step, step), step)
        sums = squares[at, :]
        for k in range(2 * NY):
            plain = rows[k, at, :].astype(F32) * inverse[k : k + 1, :]
            sums += plain * plain
        squares[at, :] = sums
        return carry

    lax.fori_loop(0, rows.shape[1] // step, body, 0)


def near_project(rows, w_up, first):
    left = jnp.concatenate([rows[k] for k in range(2 * NY)], axis=1)
    start = pl.multiple_of(first * (2 * NY * WIDTH), 2 * NY * WIDTH)
    return jnp.dot(left, w_up[pl.ds(start, 2 * NY * WIDTH), :], preferred_element_type=F32)


def expand(place, act, w_down, own, give, group):
    zl, y = place[0], place[1]
    count = act.shape[0] // 2
    for n, d in enumerate(group):
        for j in range(NY):
            start = pl.multiple_of(((zl ^ d) * NY + (y ^ j)) * WIDTH, WIDTH)
            result = jnp.dot(act[...], w_down[:, pl.ds(start, WIDTH)], preferred_element_type=F32)
            own[j][n] = result[:count]
            give[j, n] = result[count:].astype(BF16)


def first_kernel(place, *refs):
    blocks, refs = refs[: 2 * NY], refs[2 * NY :]
    w_up, w_down, total, squares, extras, next_slab, down, rows, inverse, sems, sem = refs
    later = load(place, GROUPS[1], w_up, next_slab, sems)
    whole = pltpu.make_async_copy(w_down, down, sem)
    whole.start()
    squares[...] = jnp.zeros_like(squares)
    extras[...] = jnp.zeros_like(extras)
    arrange(place, blocks, rows, inverse, extras)
    total[...] = near_project(rows, w_up, place[0] // 2)
    near_square(rows, inverse, squares)
    for copy in later:
        copy.wait()
    whole.wait()


def second_kernel(place, *refs):
    blocks, refs = refs[:8], refs[8:]
    (total_in, squares_in, extras_in, slab, w_down, act), refs = refs[:6], refs[6:]
    own, (give, extras, total, squares) = refs[:NY], refs[NY:]
    units, model = w_down.shape
    squares[...] = squares_in[...]
    extras[...] = extras_in[...]
    square(blocks, squares, extras)
    total[...] = total_in[...] + part_of(blocks, 0, slab)
    total[...] += part_of(blocks, 1, slab)
    mean = jnp.sum(squares[...], axis=1, keepdims=True) / model
    scale = lax.rsqrt(mean + 1e-05)
    act[...] = (jax.nn.silu(total[:, :units] * scale) * (total[:, units:] * scale)).astype(BF16)
    expand(place, act, w_down, own, give, GROUPS[1])


def third_kernel(place, act, w_down, *refs):
    expand(place, act, w_down, refs[:NY], refs[NY], GROUPS[0])


def call(kernel, out_shape, scratch, flops, remote, *args):
    vmem = pl.BlockSpec(memory_space=pltpu.VMEM)
    specs = [pl.BlockSpec(memory_space=pltpu.SMEM)] + [vmem] * (len(args) - 1)
    if remote:
        specs[-1] = pl.BlockSpec(memory_space=pl.ANY)
    return pl.pallas_call(
        kernel,
        out_shape=out_shape,
        in_specs=specs,
        out_specs=(vmem,) * len(out_shape),
        scratch_shapes=scratch,
        compiler_params=pltpu.CompilerParams(vmem_limit_bytes=VMEM * 1024 * 1024),
        cost_estimate=pl.CostEstimate(flops=flops, bytes_accessed=8 * 1024 * 1024, transcendentals=0),
    )(*args)


VMEM = 24
WIDTH = 256


def shapes(blocks, units):
    count = blocks[0].shape[1] - 16
    totals = ((2 * count, 2 * units), (2 * count, WIDTH))
    slab = (len(GROUPS[0]), NY * WIDTH, 2 * units)
    return count, totals, slab, 4 * count * units * NZ * NY * WIDTH


def expert_first(place, blocks, w_up, w_down):
    shape = jax.ShapeDtypeStruct
    count, totals, slab, flops = shapes(blocks, w_down.shape[0])
    out = (shape(totals[0], F32), shape(totals[1], F32), shape((16, WIDTH), F32))
    out += (shape(slab, BF16), shape(w_down.shape, BF16))
    sems = pltpu.SemaphoreType.DMA((len(GROUPS[0]) * NY,))
    scratch = [pltpu.VMEM((2 * NY, 2 * count, WIDTH), BF16), pltpu.VMEM((2 * NY, WIDTH), F32)]
    scratch += [sems, pltpu.SemaphoreType.DMA]
    return call(first_kernel, out, scratch, flops, True, place, *blocks, w_up, w_down)


def expert_rest(place, blocks, state):
    shape = jax.ShapeDtypeStruct
    units = state[-1].shape[0]
    count, totals, slab, flops = shapes(blocks, units)
    part = (len(GROUPS[0]), count, WIDTH)
    sums = (shape(part, F32),) * NY + (shape((NY,) + part, BF16),)
    act, *second, extras = call(
        second_kernel,
        (shape((2 * count, units), BF16),) + sums + (shape((16, WIDTH), F32),),
        [pltpu.VMEM(t, F32) for t in totals],
        2 * flops,
        False,
        place,
        *blocks,
        *state,
    )
    first = call(third_kernel, sums, [], flops // 2, False, place, act, state[-1])
    return first, second, extras


def split(value):
    high = lax.reduce_precision(value, 8, 7)
    return high.astype(BF16), (value - high).astype(BF16)


def slots(routes, names, capacity):
    tokens = routes.shape[0]
    chosen = jnp.sum((routes[:, :, None] == names[None, None, :]).astype(F32), axis=1)
    earlier = (jnp.arange(tokens)[:, None] > jnp.arange(tokens)[None, :]).astype(F32)
    rank = jnp.dot(earlier, chosen, preferred_element_type=F32)
    order = jnp.arange(capacity, dtype=F32)
    picks = chosen.T[:, None, :] * (rank.T[:, None, :] == order[None, :, None]).astype(F32)
    return picks.reshape(names.shape[0] * capacity, tokens)


def local(inputs, norm_gain, router, w_in, w_out, routes):
    tokens, width = inputs.shape
    experts = router.shape[1]
    capacity = min(tokens, 5 * tokens // (2 * experts))
    units = w_out.shape[1]
    model = w_in.shape[1]
    section = lax.axis_index("section")
    dp = lax.axis_index("dp")
    zl, y = section // NY, section % NY
    zh, x, core = dp // (2 * NX), dp // 2 % NX, dp % 2
    place = jnp.stack([zl, y]).astype(jnp.int32)
    w_down = w_out[0]

    acts = inputs.astype(F32)
    scaled = (acts * norm_gain).astype(BF16)
    named = jnp.zeros((16, width), BF16).at[:2, :tokens].set(routes.T.astype(BF16))
    partial_logits = lax.dot_general(
        router, scaled, (((0,), (1,)), ((), ())), preferred_element_type=F32
    )
    logit_rows = jnp.concatenate(split(partial_logits)).reshape(experts, width)
    square_row = jnp.concatenate(split(jnp.sum(acts * acts, axis=1)))[None, :]
    gain_high, _ = split(norm_gain)
    rest = norm_gain - gain_high.astype(F32)
    gain_rows = jnp.stack([gain_high, *split(rest)])
    extra = jnp.concatenate([logit_rows, square_row, gain_rows, jnp.zeros((4, width), BF16)])
    crossed = swap_h(jnp.concatenate([scaled, named], axis=0))
    near = (x + jnp.arange(NX, dtype=jnp.int32)) % NX
    names = jnp.concatenate([zh * NX + near, (zh ^ 1) * NX + near])
    picks = slots(routes, names, capacity)
    other_routes = crossed[tokens : tokens + 2, :tokens].T.astype(jnp.int32)
    other_picks = slots(other_routes, names[:NX], capacity)
    select = lambda p, v: jnp.dot(p.astype(BF16), v, preferred_element_type=F32).astype(BF16)
    mine = select(picks[: NX * capacity], scaled).reshape(NX, capacity, width)
    others = select(other_picks, crossed[:tokens]).reshape(NX, capacity, width)
    sent = jnp.stack([mine, others], axis=1)

    arrived = jnp.stack([sent[0]] + [shift_x(sent[k], k) for k in range(1, NX)])
    arrived = jnp.concatenate([arrived.reshape(NX * NH * capacity, width), extra])
    spread = [arrived] + [xor_z(arrived, d) for d in range(1, NZ)]
    blocks = []
    for group in GROUPS:
        own = jnp.stack([spread[d] for d in group])
        one, three = xor_y(own, 1), xor_y(own, 3)
        turn = jnp.where(core == 0, one, three)
        if group is GROUPS[0]:
            w_up = after(w_in, arrived)[0].reshape(model, 2 * units)
        far = far_y(turn)
        for piece in (own, one, far, three):
            if group is not GROUPS[0]:
                piece = after(piece, state[0])
            blocks += [piece, swap_core(piece)]
        if group is GROUPS[0]:
            state = expert_first(place, blocks, w_up, w_down)

    first, second, extras = expert_rest(place, blocks[8:], state)
    results = (first, second)
    sums = (extras[:4] + extras[4:8]).reshape(experts, tokens)
    inverse = lax.rsqrt((extras[8, :tokens] + extras[8, tokens:]) / model + 1e-05)
    logits = (sums * inverse[None, :]).T

    terms = [None] * NZ
    for g in (1, 0):
        *own, give = results[g]
        given = swap_core(give)
        parts = [own[j] + given[j].astype(F32) for j in range(NY)]
        passed = far_y(parts[2].astype(BF16)).astype(F32)
        one = xor_y((parts[1] + jnp.where(core == 0, passed, 0.0)).astype(BF16), 1)
        three = xor_y((parts[3] + jnp.where(core == 0, 0.0, passed)).astype(BF16), 3)
        column = parts[0] + one.astype(F32) + three.astype(F32)
        for n, d in enumerate(GROUPS[g]):
            terms[d] = xor_z(column[n].astype(BF16), d).astype(F32) if d else column[n]
    full = sum(terms[1:], terms[0]).astype(BF16).reshape(NX, NH, capacity, width)
    back = jnp.stack([full[0]] + [shift_x(full[k], -k) for k in range(1, NX)], axis=1)
    back = jnp.concatenate([back[0], swap_h(back[1])]).reshape(experts * capacity, width)

    hits = (routes[:, :, None] == names[None, None, :]).astype(F32)
    table = (routes[:, :, None] == jnp.arange(experts)[None, None, :]).astype(F32)
    gates = jax.nn.softmax(jnp.sum(table * logits[:, None, :], axis=2), axis=1)
    gate_of = jnp.sum(hits * gates[:, :, None], axis=1)
    weight = jnp.repeat(gate_of.T, capacity, axis=0) * picks
    high, low = split(weight)
    mix = lambda w: lax.dot_general(w, back, (((0,), (0,)), ((), ())), preferred_element_type=F32)
    return (acts + (mix(high) + mix(low))).astype(BF16)


def solution(mesh):
    return jax.shard_map(
        local,
        mesh=mesh,
        in_specs=(
            P("dp", "section"),
            P("section"),
            P("section", None),
            P("dp", None, None, "section"),
            P("dp", "section", None),
            P("dp", None),
        ),
        out_specs=P("dp", "section"),
        check_vma=False,
    )
```
